32 devices in a mesh: row: 8 (over y, x, core), col: 4 (over z).
Axes of the slice: x: 2, y: 2, z: 4, core: 2. Of those that a mesh axis runs over, the one named last changes fastest.
Arguments:
- matrix: float32 [16384, 5, 4, 128], P('row', None, 'col'), may hold values from -320 to 320, as said below
Outputs:
- r_rows: float32 [256, 5, 4, 128], P(None, None, 'col')
- residual: float32 [16384, 5, 4, 128], P('row', None, 'col')
The draws below stay inside these ranges and needn't reach their ends.
Inputs may be any that keep to these rules, and one draw needn't show every extreme that they name: `matrix`: real entries; the first 256 columns have full column rank on every block of 2048 rows.
All inputs are finite; a program needn't handle non-finite values.
Results may differ from the reference program's by a relative error of at most 0.0003.
Values sent between devices are 32-bit elements; how exact they have to be, the bound alone decides.
A program may use at most 128 MiB of HBM per device.

```python
import math
import jax
import jax.numpy as jnp
from jax import lax

BLK = 128
PANEL = 256
CB = 5
ROWS = 16384
N_COL = 4


def draw_matrix(key, part):
    key_base = jax.random.fold_in(key, 11)
    key_gain = jax.random.fold_in(key, 12)
    key_scale = jax.random.fold_in(key, 13)
    shape = (ROWS, CB, N_COL, BLK)
    base = jax.random.truncated_normal(key_base, -4.0, 4.0, shape, jnp.float32)
    first = base[:, 0, 0:2, :].reshape(ROWS, PANEL)
    mixed = first + 0.6 * jnp.roll(first, -1, axis=1)
    mixed_blocks = mixed.reshape(ROWS, 2, BLK)
    parity = jnp.arange(N_COL) % 2
    spread = mixed_blocks[:, parity, :][:, None, :, :]
    gains = jax.random.uniform(key_gain, (CB, N_COL, BLK), jnp.float32, -1.0, 1.0)
    full = base + gains[None] * spread
    full = full.at[:, 0, 0:2, :].set(mixed_blocks)
    rising = jnp.arange(ROWS, dtype=jnp.float32) / ROWS
    jitter = jax.random.uniform(key_scale, (ROWS,), jnp.float32, 0.0, 1.0)
    scales = jnp.exp(math.log(3.0) * rising + math.log(10.0) * jitter)
    return (full * scales[:, None, None, None]).astype(jnp.float32)


def setup_inputs(seed: int = 0) -> dict:
    keys = jax.random.split(jax.random.key(seed), 2)
    return {
        "matrix": draw_matrix(jax.random.fold_in(keys[1], 71), 0),
    }


def reference(matrix):
    flat = matrix.reshape(ROWS, CB * N_COL * BLK)
    panel = flat[:, :PANEL]
    basis, upper = jnp.linalg.qr(panel)
    signs = jnp.where(jnp.diagonal(upper) < 0, -1.0, 1.0)
    basis = basis * signs[None, :]
    top = jnp.dot(basis.T, flat, precision=lax.Precision.HIGHEST)
    residual = flat - jnp.dot(basis, top, precision=lax.Precision.HIGHEST)
    scaled = top / math.sqrt(ROWS)
    return (scaled.reshape(PANEL, CB, N_COL, BLK), residual.reshape(ROWS, CB, N_COL, BLK))
```

```python
import functools
import math

import jax
import jax.numpy as jnp
from jax import lax
from jax.experimental import pallas as pl
from jax.experimental.pallas import tpu as pltpu
from jax.sharding import PartitionSpec as P

VMEM_LIMIT = 48 * 1024 * 1024
LANES = 128


def dot_exact(left, right, contract_left, contract_right):
    return lax.dot_general(
        left,
        right,
        (((contract_left,), (contract_right,)), ((), ())),
        precision=lax.Precision.HIGHEST,
        preferred_element_type=jnp.float32,
    )


def split(value):
    high = value.astype(jnp.bfloat16)
    low = (value - high.astype(jnp.float32)).astype(jnp.bfloat16)
    return high, low


def dot_split(left, right):
    left_high, left_low = left
    right_high, right_low = right
    dot = functools.partial(jnp.dot, preferred_element_type=jnp.float32)
    return dot(left_high, right_high) + (dot(left_high, right_low) + dot(left_low, right_high))


def lower_inverse(block):
    size = block.shape[0]
    row = lax.broadcasted_iota(jnp.int32, (size, 1), 0)
    row8 = lax.broadcasted_iota(jnp.int32, (8, 1), 0)
    eye = (
        lax.broadcasted_iota(jnp.int32, (size, size), 0)
        == lax.broadcasted_iota(jnp.int32, (size, size), 1)
    ).astype(jnp.float32)

    def group(step, carry):
        left, right = carry
        limit = size - 8 * step
        for j in range(8):
            pivot = left[j : j + 1, j : j + 1]
            root = lax.rsqrt(pivot)
            root = root * (1.5 - 0.5 * (pivot * root) * root)
            left_row = left[j : j + 1, :] * root
            right_row = right[j : j + 1, :] * root
            factor = jnp.where((row > j) & (row < limit), left[:, j : j + 1] * root, 0.0)
            left = left - factor * left_row
            right = right - factor * right_row
            head = jnp.where(row8 == j, right_row, right[:8])
            right = jnp.concatenate([head, right[8:]], axis=0)
        left = jnp.concatenate([left[8:], left[:8]], axis=0)
        left = pltpu.roll(left, size - 8, 1)
        right = jnp.concatenate([right[8:], right[:8]], axis=0)
        return left, right

    return lax.fori_loop(0, size // 8, group, (block, eye))[1]


def factor_into(top_left, top_right, bottom_right, out_ref):
    first = lower_inverse(top_left)
    coupling = dot_exact(first, top_right, 1, 0)
    schur = bottom_right - dot_exact(coupling, coupling, 0, 0)
    second = lower_inverse(schur)
    corner = -dot_exact(second, dot_exact(coupling, first, 0, 0), 1, 0)
    half = top_left.shape[0]
    out_ref[:half, :half] = first
    out_ref[:half, half:] = jnp.zeros_like(first)
    out_ref[half:, :half] = corner
    out_ref[half:, half:] = second


def update_kernel(
    scale, chunk, matrix, panel, summed, inverse, r_rows, residual,
    local, wide, result, top_buf, load_sem, panel_sem, store_sem, top_sem,
):
    rows = matrix.shape[0]
    blocks = matrix.shape[1]
    count = rows // chunk

    def span(c):
        return pl.ds(c * chunk, chunk)

    def load(c, b):
        return pltpu.make_async_copy(
            matrix.at[span(c), b, 0, :], local.at[b, span(c), :], load_sem.at[c, b]
        )

    def load_panel(c, h):
        return pltpu.make_async_copy(
            panel.at[h, span(c), :], wide.at[h, span(c), :], panel_sem.at[c, h]
        )

    def store(c, b):
        return pltpu.make_async_copy(
            result.at[b, span(c), :], residual.at[span(c), b, 0, :], store_sem.at[c, b]
        )

    def store_top(b):
        return pltpu.make_async_copy(top_buf.at[b], r_rows.at[:, b, 0, :], top_sem.at[b])

    for c in range(count):
        for h in range(2):
            load_panel(c, h).start()
        for b in range(blocks):
            load(c, b).start()
    top = dot_exact(inverse[...], summed[...], 1, 0)
    for b in range(blocks):
        top_buf[b] = top[:, b * LANES : (b + 1) * LANES] * scale
        store_top(b).start()
    weights = split(dot_exact(inverse[...], top, 0, 0))
    for c in range(count):
        for h in range(2):
            load_panel(c, h).wait()
        for b in range(blocks):
            load(c, b).wait()
        rows_c = slice(c * chunk, (c + 1) * chunk)
        left = split(jnp.concatenate([wide[0, rows_c, :], wide[1, rows_c, :]], axis=1))
        product = dot_split(left, weights)
        for b in range(blocks):
            result[b, rows_c, :] = local[b, rows_c, :] - product[:, b * LANES : (b + 1) * LANES]
            store(c, b).start()
    for b in range(blocks):
        store_top(b).wait()
        for c in range(count):
            store(c, b).wait()


def update(matrix, panel, summed, inverse, total_rows):
    rows, blocks, _, width = matrix.shape
    chunk = 256
    count = rows // chunk
    names = pltpu.SemaphoreType.DMA
    vmem = pl.BlockSpec(memory_space=pltpu.VMEM)
    hbm = pl.BlockSpec(memory_space=pl.ANY)
    return pl.pallas_call(
        functools.partial(update_kernel, 1.0 / math.sqrt(total_rows), chunk),
        out_shape=(
            jax.ShapeDtypeStruct((2 * width, blocks, 1, width), jnp.float32),
            jax.ShapeDtypeStruct(matrix.shape, jnp.float32),
        ),
        in_specs=[hbm, hbm, vmem, vmem],
        out_specs=(hbm, hbm),
        scratch_shapes=[
            pltpu.VMEM((blocks, rows, width), jnp.float32),
            pltpu.VMEM((2, rows, width), jnp.float32),
            pltpu.VMEM((blocks, rows, width), jnp.float32),
            pltpu.VMEM((blocks, 2 * width, width), jnp.float32),
            names((count, blocks)),
            names((count, 2)),
            names((count, blocks)),
            names((blocks,)),
        ],
        compiler_params=pltpu.CompilerParams(vmem_limit_bytes=VMEM_LIMIT),
        name="update",
    )(matrix, panel, summed, inverse)


def factor_kernel(gram, out):
    factor_into(
        gram[:LANES, :LANES], gram[:LANES, LANES:], gram[LANES:, LANES:], out
    )


def factor(gram):
    vmem = pl.BlockSpec(memory_space=pltpu.VMEM)
    return pl.pallas_call(
        factor_kernel,
        out_shape=jax.ShapeDtypeStruct(gram.shape, jnp.float32),
        in_specs=[vmem],
        out_specs=vmem,
        compiler_params=pltpu.CompilerParams(vmem_limit_bytes=VMEM_LIMIT),
        name="factor",
    )(gram)


def per_device(matrix):
    rows, blocks, _, width = matrix.shape
    me = lax.axis_index("col")
    n_col = lax.axis_size("col")
    own = matrix[:, 0, 0, :]
    chain = [(i, i + 1) for i in range(n_col - 1)]
    back = lax.ppermute(own, "col", [(1, 0)])
    first = second = own
    first = jnp.where(me == 1, back, own)
    second = jnp.where(me == 0, back, own)
    moving = own
    for step in range(1, n_col):
        moving = lax.ppermute(moving, "col", chain)
        first = jnp.where(me == step, moving, first)
        second = jnp.where(me == step + 1, moving, second)
    panel = jnp.stack([first, second])
    pair = jnp.concatenate([first, second], axis=1)
    local = matrix.reshape(rows, blocks * width)
    both = dot_exact(pair, jnp.concatenate([pair, local], axis=1), 0, 0)
    both = lax.psum(both, "row")
    inverse = factor(both[:, : 2 * width])
    total_rows = rows * lax.axis_size("row")
    return update(matrix, panel, both[:, 2 * width :], inverse, total_rows)


def solution(mesh):
    return jax.shard_map(
        per_device,
        mesh=mesh,
        in_specs=(P("row", None, "col", None),),
        out_specs=(P(None, None, "col", None), P("row", None, "col", None)),
        check_vma=False,
    )
```

```python
import functools
import math

import jax
import jax.numpy as jnp
from jax import lax
from jax.experimental import pallas as pl
from jax.experimental.pallas import tpu as pltpu
from jax.sharding import PartitionSpec as P

VMEM_LIMIT = 48 * 1024 * 1024
LANES = 128


def dot_exact(left, right, contract_left, contract_right):
    return lax.dot_general(
        left,
        right,
        (((contract_left,), (contract_right,)), ((), ())),
        precision=lax.Precision.HIGHEST,
        preferred_element_type=jnp.float32,
    )


def split(value):
    high = value.astype(jnp.bfloat16)
    low = (value - high.astype(jnp.float32)).astype(jnp.bfloat16)
    return high, low


def dot_split(left, right):
    left_high, left_low = left
    right_high, right_low = right
    dot = functools.partial(jnp.dot, preferred_element_type=jnp.float32)
    return dot(left_high, right_high) + (dot(left_high, right_low) + dot(left_low, right_high))


def lower_inverse(block):
    size = block.shape[0]
    row = lax.broadcasted_iota(jnp.int32, (size, 1), 0)
    row8 = lax.broadcasted_iota(jnp.int32, (8, 1), 0)
    eye = (
        lax.broadcasted_iota(jnp.int32, (size, size), 0)
        == lax.broadcasted_iota(jnp.int32, (size, size), 1)
    ).astype(jnp.float32)

    def group(step, carry):
        left, right = carry
        limit = size - 8 * step
        for j in range(8):
            pivot = left[j : j + 1, j : j + 1]
            root = lax.rsqrt(pivot)
            root = root * (1.5 - 0.5 * (pivot * root) * root)
            left_row = left[j : j + 1, :] * root
            right_row = right[j : j + 1, :] * root
            factor = jnp.where((row > j) & (row < limit), left[:, j : j + 1] * root, 0.0)
            left = left - factor * left_row
            right = right - factor * right_row
            head = jnp.where(row8 == j, right_row, right[:8])
            right = jnp.concatenate([head, right[8:]], axis=0)
        left = jnp.concatenate([left[8:], left[:8]], axis=0)
        left = pltpu.roll(left, size - 8, 1)
        right = jnp.concatenate([right[8:], right[:8]], axis=0)
        return left, right

    return lax.fori_loop(0, size // 8, group, (block, eye))[1]


def update_kernel(
    scale, chunk, matrix, panel, summed, inverse, r_rows, residual,
    local, wide, result, top_buf, load_sem, panel_sem, store_sem, top_sem,
):
    rows = matrix.shape[0]
    blocks = matrix.shape[1]
    count = rows // chunk

    def span(c):
        return pl.ds(c * chunk, chunk)

    def load(c, b):
        return pltpu.make_async_copy(
            matrix.at[span(c), b, 0, :], local.at[b, span(c), :], load_sem.at[c, b]
        )

    def load_panel(c, h):
        return pltpu.make_async_copy(
            panel.at[h, span(c), :], wide.at[h, span(c), :], panel_sem.at[c, h]
        )

    def store(c, b):
        return pltpu.make_async_copy(
            result.at[b, span(c), :], residual.at[span(c), b, 0, :], store_sem.at[c, b]
        )

    def store_top(b):
        return pltpu.make_async_copy(top_buf.at[b], r_rows.at[:, b, 0, :], top_sem.at[b])

    for c in range(count):
        for h in range(2):
            load_panel(c, h).start()
        for b in range(blocks):
            load(c, b).start()
    top = dot_exact(inverse[...], summed[...], 1, 0)
    for b in range(blocks):
        top_buf[b] = top[:, b * LANES : (b + 1) * LANES] * scale
        store_top(b).start()
    weights = split(dot_exact(inverse[...], top, 0, 0))
    for c in range(count):
        for h in range(2):
            load_panel(c, h).wait()
        for b in range(blocks):
            load(c, b).wait()
        rows_c = slice(c * chunk, (c + 1) * chunk)
        left = split(jnp.concatenate([wide[0, rows_c, :], wide[1, rows_c, :]], axis=1))
        product = dot_split(left, weights)
        for b in range(blocks):
            result[b, rows_c, :] = local[b, rows_c, :] - product[:, b * LANES : (b + 1) * LANES]
            store(c, b).start()
    for b in range(blocks):
        store_top(b).wait()
        for c in range(count):
            store(c, b).wait()


def update(matrix, panel, summed, inverse, total_rows):
    rows, blocks, _, width = matrix.shape
    chunk = 256
    count = rows // chunk
    names = pltpu.SemaphoreType.DMA
    vmem = pl.BlockSpec(memory_space=pltpu.VMEM)
    hbm = pl.BlockSpec(memory_space=pl.ANY)
    return pl.pallas_call(
        functools.partial(update_kernel, 1.0 / math.sqrt(total_rows), chunk),
        out_shape=(
            jax.ShapeDtypeStruct((2 * width, blocks, 1, width), jnp.float32),
            jax.ShapeDtypeStruct(matrix.shape, jnp.float32),
        ),
        in_specs=[hbm, hbm, vmem, vmem],
        out_specs=(hbm, hbm),
        scratch_shapes=[
            pltpu.VMEM((blocks, rows, width), jnp.float32),
            pltpu.VMEM((2, rows, width), jnp.float32),
            pltpu.VMEM((blocks, rows, width), jnp.float32),
            pltpu.VMEM((blocks, 2 * width, width), jnp.float32),
            names((count, blocks)),
            names((count, 2)),
            names((count, blocks)),
            names((blocks,)),
        ],
        compiler_params=pltpu.CompilerParams(vmem_limit_bytes=VMEM_LIMIT),
        name="update",
    )(matrix, panel, summed, inverse)

def stream_kernel(
    n_row, n_col, owners, chunk, matrix, panel, summed, inverse,
    local, wide, work, total, gram, gram_total, slots, gram_slots, factors,
    load_sem, own_sem, out_sem, recv_sem, send_sem, factor_recv, factor_send,
    scatter_send, scatter_recv, gather_send, gather_recv,
):
    rows, blocks = matrix.shape[0], matrix.shape[1]
    count = rows // chunk
    piece = LANES // owners
    row = lax.axis_index("row")
    col = lax.axis_index("col")
    has_right = col < n_col - 1

    def span(c):
        return pl.ds(pl.multiple_of(c * chunk, chunk), chunk)

    def remote(source, target, sent, received, to_row, to_col):
        return pltpu.make_async_remote_copy(
            src_ref=source,
            dst_ref=target,
            send_sem=sent,
            recv_sem=received,
            device_id={"row": to_row, "col": to_col},
            device_id_type=pl.DeviceIdType.MESH,
        )

    def send(way, half, c):
        place = wide.at[half, span(c), :]
        to_col = col + 1 if way == 0 else col - 1
        return remote(
            place, place, send_sem.at[way, half, c], recv_sem.at[half, c], row, to_col
        )

    def send_factor(which):
        place = factors.at[which]
        return remote(
            place, place, factor_send.at[which], factor_recv.at[which], row, col + 1
        )

    def load(b):
        return pltpu.make_async_copy(matrix.at[:, b, 0, :], local.at[b], load_sem.at[b])

    def load_own(half):
        return pltpu.make_async_copy(matrix.at[:, 0, 0, :], wide.at[half], own_sem)

    def store_panel(half):
        return pltpu.make_async_copy(wide.at[half], panel.at[half], out_sem.at[half])

    def source_of(stage, owner):
        start = pl.multiple_of(owner * piece, 8)
        if stage == 2:
            return gram.at[pl.ds(start, piece), :]
        return work.at[pl.ds(stage * LANES + start, piece), :]

    def total_of(stage, owner):
        start = pl.multiple_of(owner * piece, 8)
        if stage == 2:
            return gram_total.at[pl.ds(start, piece), :]
        return total.at[pl.ds(stage * LANES + start, piece), :]

    def slot_of(stage, d):
        return gram_slots.at[d] if stage == 2 else slots.at[stage, d]

    def scatter(stage, d):
        owner = lax.rem(row + d, n_row)
        copy = remote(
            source_of(stage, owner), slot_of(stage, d),
            scatter_send.at[stage, d], scatter_recv.at[stage, d], owner, col,
        )
        return owner, copy

    def gather(stage, d):
        other = lax.rem(row + d, n_row)
        place = total_of(stage, row)
        return remote(
            place, place, gather_send.at[stage, d], gather_recv.at[stage, d], other, col
        )

    def scatter_start(stage):
        @pl.loop(1, n_row)
        def _(d):
            owner, copy = scatter(stage, d)
            pl.when(owner < owners)(copy.start)

    def scatter_finish(stage):
        @pl.when(row < owners)
        def _():
            @pl.loop(1, n_row)
            def _(d):
                slot = slot_of(stage, d)
                remote(
                    slot, slot, scatter_send.at[stage, d], scatter_recv.at[stage, d], row, col
                ).wait_recv()

            value = source_of(stage, row)[...]
            for d in range(1, n_row):
                value = value + slot_of(stage, d)[...]
            total_of(stage, row)[...] = value

            @pl.loop(1, n_row)
            def _(d):
                gather(stage, d).start()

    def gather_finish(stage):
        @pl.loop(1, n_row)
        def _(d):
            other = lax.rem(row - d + n_row, n_row)

            @pl.when(other < owners)
            def _():
                place = total_of(stage, other)
                remote(
                    place, place, gather_send.at[stage, d], gather_recv.at[stage, d], row, col
                ).wait_recv()

    def settle(stage):
        @pl.loop(1, n_row)
        def _(d):
            owner, copy = scatter(stage, d)
            pl.when(owner < owners)(copy.wait_send)
            pl.when(row < owners)(gather(stage, d).wait_send)

    def window(c):
        return jnp.concatenate([local[b, span(c), :] for b in range(blocks)], axis=1)

    for half in range(2):
        pl.when(col == half)(load_own(half).start)
    for b in range(blocks):
        load(b).start()

    barrier = pltpu.get_barrier_semaphore()

    def greet(to_row, to_col):
        pl.semaphore_signal(
            barrier,
            inc=1,
            device_id={"row": to_row, "col": to_col},
            device_id_type=pl.DeviceIdType.MESH,
        )

    for d in range(1, n_row):
        greet(lax.rem(row + d, n_row), col)
    pl.when(col > 0)(lambda: greet(row, col - 1))
    pl.when(has_right)(lambda: greet(row, col + 1))
    work[...] = jnp.zeros_like(work)
    gram[...] = jnp.zeros_like(gram)
    inner = (col > 0) & has_right
    pl.semaphore_wait(barrier, n_row + inner.astype(jnp.int32))

    @pl.when(col < 2)
    def _():
        load_own(0).wait()

    @pl.when(col == 0)
    def _():
        @pl.loop(0, count)
        def _(c):
            send(0, 0, c).start()

    @pl.when(col == 1)
    def _():
        @pl.loop(0, count)
        def _(c):
            if n_col > 2:
                send(0, 1, c).start()
            send(1, 1, c).start()

    for b in range(blocks):
        load(b).wait()

    @pl.when(col < 2)
    def _():
        @pl.loop(0, count)
        def _(c):
            send(0, 1 - col, c).wait_recv()

            if n_col > 2:

                @pl.when((col == 1) & (c >= count // 2))
                def _():
                    send(0, 0, 2 * c - count).start()
                    send(0, 0, 2 * c - count + 1).start()

            pair = jnp.concatenate([wide[0, span(c), :], wide[1, span(c), :]], axis=1)
            cross = dot_exact(pair, pair, 0, 0)
            gram[...] += jnp.concatenate([cross[:LANES], cross[LANES:]], axis=1)
            work[...] += dot_exact(pair, window(c), 0, 0)

        scatter_start(2)
        for half in range(2):
            store_panel(half).start()
        scatter_start(1)
        scatter_finish(2)
        scatter_start(0)
        gather_finish(2)
        first = lower_inverse(gram_total[:, :LANES])
        factors[0] = first

        if n_col > 2:
            pl.when(col == 1)(send_factor(0).start)
        coupling = dot_exact(first, gram_total[:, LANES : 2 * LANES], 1, 0)
        schur = gram_total[:, 3 * LANES :] - dot_exact(coupling, coupling, 0, 0)
        carried = dot_exact(coupling, first, 0, 0)
        second = lower_inverse(schur)
        factors[1] = second
        if n_col > 2:
            pl.when(col == 1)(send_factor(1).start)
        factors[2] = -dot_exact(second, carried, 1, 0)
        if n_col > 2:
            pl.when(col == 1)(send_factor(2).start)
        scatter_finish(1)
        scatter_finish(0)
        gather_finish(1)
        gather_finish(0)
        for half in range(2):
            store_panel(half).wait()
        for stage in (2, 1, 0):
            settle(stage)

        @pl.loop(0, count)
        def _(c):
            @pl.when(col == 0)
            def _():
                send(0, 0, c).wait_send()

            @pl.when(col == 1)
            def _():
                send(1, 1, c).wait_send()
                if n_col > 2:
                    send(0, 1, c).wait_send()
                    send(0, 0, c).wait_send()

        if n_col > 2:

            @pl.when(col == 1)
            def _():
                for which in range(3):
                    send_factor(which).wait_send()

    if n_col > 2:

        @pl.when(col >= 2)
        def _():
            for half in (1, 0):

                @pl.loop(0, count)
                def _(c):
                    send(0, half, c).wait_recv()
                    pl.when(has_right)(send(0, half, c).start)
                    if half == 0:
                        pl.when(c == count // 2)(lambda: scatter_finish(1))
                    here = pl.ds(half * LANES, LANES)
                    work[here, :] += dot_exact(wide[half, span(c), :], window(c), 0, 0)

                scatter_start(half)
                store_panel(half).start()

            scatter_finish(0)
            for which in range(3):
                send_factor(which).wait_recv()
                pl.when(has_right)(send_factor(which).start)
            gather_finish(1)
            gather_finish(0)
            for half in range(2):
                store_panel(half).wait()
            for stage in (1, 0):
                settle(stage)

            @pl.when(has_right)
            def _():
                @pl.loop(0, count)
                def _(c):
                    for half in range(2):
                        send(0, half, c).wait_send()

                for which in range(3):
                    send_factor(which).wait_send()

    summed[...] = total[...]
    inverse[:LANES, :LANES] = factors[0]
    inverse[:LANES, LANES:] = jnp.zeros((LANES, LANES), jnp.float32)
    inverse[LANES:, :LANES] = factors[2]
    inverse[LANES:, LANES:] = factors[1]


def stream(matrix):
    rows, blocks, _, width = matrix.shape
    n_row = lax.axis_size("row")
    n_col = lax.axis_size("col")
    owners = min(n_row, 16)
    piece = LANES // owners
    chunk = 256
    count = rows // chunk
    columns = blocks * width
    sem = pltpu.SemaphoreType.DMA
    vmem = pl.BlockSpec(memory_space=pltpu.VMEM)
    hbm = pl.BlockSpec(memory_space=pl.ANY)

    def floats(*shape):
        return pltpu.VMEM(shape, jnp.float32)

    return pl.pallas_call(
        functools.partial(stream_kernel, n_row, n_col, owners, chunk),
        out_shape=(
            jax.ShapeDtypeStruct((2, rows, width), jnp.float32),
            jax.ShapeDtypeStruct((2 * width, columns), jnp.float32),
            jax.ShapeDtypeStruct((2 * width, 2 * width), jnp.float32),
        ),
        in_specs=[hbm],
        out_specs=(hbm, vmem, vmem),
        scratch_shapes=[
            floats(blocks, rows, width),
            floats(2, rows, width),
            floats(2 * width, columns),
            floats(2 * width, columns),
            floats(width, 4 * width),
            floats(width, 4 * width),
            floats(2, n_row, piece, columns),
            floats(n_row, piece, 4 * width),
            floats(3, width, width),
            sem((blocks,)),
            sem,
            sem((2,)),
            sem((2, count)),
            sem((2, 2, count)),
            sem((3,)),
            sem((3,)),
            sem((3, n_row)),
            sem((3, n_row)),
            sem((3, n_row)),
            sem((3, n_row)),
        ],
        compiler_params=pltpu.CompilerParams(
            collective_id=0, has_side_effects=True, vmem_limit_bytes=VMEM_LIMIT
        ),
        name="stream",
    )(matrix)


def per_device(matrix):
    panel, summed, inverse = stream(matrix)
    total_rows = matrix.shape[0] * lax.axis_size("row")
    return update(matrix, panel, summed, inverse, total_rows)


def solution(mesh):
    return jax.shard_map(
        per_device,
        mesh=mesh,
        in_specs=(P("row", None, "col", None),),
        out_specs=(P(None, None, "col", None), P("row", None, "col", None)),
        check_vma=False,
    )
```

```python
import functools
import math

import jax
import jax.numpy as jnp
from jax import lax
from jax.experimental import pallas as pl
from jax.experimental.pallas import tpu as pltpu
from jax.sharding import PartitionSpec as P

VMEM_LIMIT = 32 * 1024 * 1024
STREAM_VMEM_LIMIT = 52 * 1024 * 1024
LANES = 128


def dot_exact(left, right, contract_left, contract_right):
    return lax.dot_general(
        left,
        right,
        (((contract_left,), (contract_right,)), ((), ())),
        precision=lax.Precision.HIGHEST,
        preferred_element_type=jnp.float32,
    )


def split(value):
    high = value.astype(jnp.bfloat16)
    low = (value - high.astype(jnp.float32)).astype(jnp.bfloat16)
    return high, low


def dot_split(left, right):
    left_high, left_low = left
    right_high, right_low = right
    dot = functools.partial(jnp.dot, preferred_element_type=jnp.float32)
    return dot(left_high, right_high) + (dot(left_high, right_low) + dot(left_low, right_high))


def lower_inverse(block):
    size = block.shape[0]
    row = lax.broadcasted_iota(jnp.int32, (size, 1), 0)
    row8 = lax.broadcasted_iota(jnp.int32, (8, 1), 0)
    eye = (
        lax.broadcasted_iota(jnp.int32, (size, size), 0)
        == lax.broadcasted_iota(jnp.int32, (size, size), 1)
    ).astype(jnp.float32)

    def group(step, carry):
        left, right = carry
        limit = size - 8 * step
        for j in range(8):
            pivot = left[j : j + 1, j : j + 1]
            root = lax.rsqrt(pivot)
            root = root * (1.5 - 0.5 * (pivot * root) * root)
            left_row = left[j : j + 1, :] * root
            right_row = right[j : j + 1, :] * root
            factor = jnp.where((row > j) & (row < limit), left[:, j : j + 1] * root, 0.0)
            left = left - factor * left_row
            right = right - factor * right_row
            head = jnp.where(row8 == j, right_row, right[:8])
            right = jnp.concatenate([head, right[8:]], axis=0)
        left = jnp.concatenate([left[8:], left[:8]], axis=0)
        left = pltpu.roll(left, size - 8, 1)
        right = jnp.concatenate([right[8:], right[:8]], axis=0)
        return left, right

    return lax.fori_loop(0, size // 8, group, (block, eye))[1]


def update_kernel(
    scale, chunk, local, wide, summed, inverse, r_rows, residual,
    result, top_buf, store_sem, top_sem,
):
    blocks, rows = local.shape[0], local.shape[1]
    count = rows // chunk

    def store(c, b):
        span = pl.ds(c * chunk, chunk)
        return pltpu.make_async_copy(
            result.at[b, span, :], residual.at[span, b, 0, :], store_sem.at[c, b]
        )

    def store_top(b):
        return pltpu.make_async_copy(top_buf.at[b], r_rows.at[:, b, 0, :], top_sem.at[b])

    top = dot_exact(inverse[...], summed[...], 1, 0)
    weights = split(dot_exact(inverse[...], top, 0, 0))
    for c in range(count):
        rows_c = slice(c * chunk, (c + 1) * chunk)
        left = split(jnp.concatenate([wide[0, rows_c, :], wide[1, rows_c, :]], axis=1))
        product = dot_split(left, weights)
        for b in range(blocks):
            result[b, rows_c, :] = local[b, rows_c, :] - product[:, b * LANES : (b + 1) * LANES]
            store(c, b).start()
    for b in range(blocks):
        top_buf[b] = top[:, b * LANES : (b + 1) * LANES] * scale
        store_top(b).start()
    for b in range(blocks):
        store_top(b).wait()
        for c in range(count):
            store(c, b).wait()


def update(local, panel, summed, inverse, total_rows):
    blocks, rows, width = local.shape
    chunk = 256
    count = rows // chunk
    sem = pltpu.SemaphoreType.DMA
    vmem = pl.BlockSpec(memory_space=pltpu.VMEM)
    hbm = pl.BlockSpec(memory_space=pl.ANY)
    return pl.pallas_call(
        functools.partial(update_kernel, 1.0 / math.sqrt(total_rows), chunk),
        out_shape=(
            jax.ShapeDtypeStruct((2 * width, blocks, 1, width), jnp.float32),
            jax.ShapeDtypeStruct((rows, blocks, 1, width), jnp.float32),
        ),
        in_specs=[vmem] * 4,
        out_specs=(hbm, hbm),
        scratch_shapes=[
            pltpu.VMEM((blocks, rows, width), jnp.float32),
            pltpu.VMEM((blocks, 2 * width, width), jnp.float32),
            sem((count, blocks)),
            sem((blocks,)),
        ],
        compiler_params=pltpu.CompilerParams(vmem_limit_bytes=VMEM_LIMIT),
        name="update",
    )(local, panel, summed, inverse)


def stream_kernel(
    n_row, n_col, owners, chunk, matrix, local, panel, summed, inverse,
    wide, work, total, gram, gram_total, slots, gram_slots, factors,
    load_sem, own_sem, out_sem, recv_sem, send_sem, factor_recv, factor_send,
    scatter_send, scatter_recv, gather_send, gather_recv,
):
    rows, blocks = matrix.shape[0], matrix.shape[1]
    count = rows // chunk
    piece = LANES // owners
    row = lax.axis_index("row")
    col = lax.axis_index("col")
    has_right = col < n_col - 1

    def span(c):
        return pl.ds(pl.multiple_of(c * chunk, chunk), chunk)

    def remote(source, target, sent, received, to_row, to_col):
        return pltpu.make_async_remote_copy(
            src_ref=source,
            dst_ref=target,
            send_sem=sent,
            recv_sem=received,
            device_id={"row": to_row, "col": to_col},
            device_id_type=pl.DeviceIdType.MESH,
        )

    def send(way, half, c):
        place = wide.at[half, span(c), :]
        to_col = col + 1 if way == 0 else col - 1
        return remote(
            place, place, send_sem.at[way, half, c], recv_sem.at[half, c], row, to_col
        )

    def send_factor(which):
        place = factors.at[which]
        return remote(
            place, place, factor_send.at[which], factor_recv.at[which], row, col + 1
        )

    def load(b):
        return pltpu.make_async_copy(matrix.at[:, b, 0, :], local.at[b], load_sem.at[b])

    def load_own(half):
        return pltpu.make_async_copy(matrix.at[:, 0, 0, :], wide.at[half], own_sem)

    def store_panel(half):
        return pltpu.make_async_copy(wide.at[half], panel.at[half], out_sem.at[half])

    def source_of(stage, owner):
        start = pl.multiple_of(owner * piece, 8)
        if stage >= 2:
            return gram.at[stage - 2, pl.ds(start, piece), :]
        return work.at[pl.ds(stage * LANES + start, piece), :]

    def total_of(stage, owner):
        start = pl.multiple_of(owner * piece, 8)
        if stage >= 2:
            return gram_total.at[stage - 2, pl.ds(start, piece), :]
        return total.at[pl.ds(stage * LANES + start, piece), :]

    def slot_of(stage, d):
        return gram_slots.at[stage - 2, d] if stage >= 2 else slots.at[stage, d]

    def scatter(stage, d):
        owner = lax.rem(row + d, n_row)
        copy = remote(
            source_of(stage, owner), slot_of(stage, d),
            scatter_send.at[stage, d], scatter_recv.at[stage, d], owner, col,
        )
        return owner, copy

    def gather(stage, d):
        other = lax.rem(row + d, n_row)
        place = total_of(stage, row)
        return remote(
            place, place, gather_send.at[stage, d], gather_recv.at[stage, d], other, col
        )

    def scatter_start(stage):
        @pl.loop(1, n_row)
        def _(d):
            owner, copy = scatter(stage, d)
            pl.when(owner < owners)(copy.start)

    def scatter_finish(stage):
        @pl.when(row < owners)
        def _():
            @pl.loop(1, n_row)
            def _(d):
                slot = slot_of(stage, d)
                remote(
                    slot, slot, scatter_send.at[stage, d], scatter_recv.at[stage, d], row, col
                ).wait_recv()

            value = source_of(stage, row)[...]
            for d in range(1, n_row):
                value = value + slot_of(stage, d)[...]
            total_of(stage, row)[...] = value

            @pl.loop(1, n_row)
            def _(d):
                gather(stage, d).start()

    def gather_finish(stage):
        @pl.loop(1, n_row)
        def _(d):
            other = lax.rem(row - d + n_row, n_row)

            @pl.when(other < owners)
            def _():
                place = total_of(stage, other)
                remote(
                    place, place, gather_send.at[stage, d], gather_recv.at[stage, d], row, col
                ).wait_recv()

    def settle(stage):
        @pl.loop(1, n_row)
        def _(d):
            owner, copy = scatter(stage, d)
            pl.when(owner < owners)(copy.wait_send)
            pl.when(row < owners)(gather(stage, d).wait_send)

    def window(c):
        return jnp.concatenate([local[b, span(c), :] for b in range(blocks)], axis=1)

    for half in range(2):
        pl.when(col == half)(load_own(half).start)
    for b in range(blocks):
        load(b).start()

    barrier = pltpu.get_barrier_semaphore()

    def greet(to_row, to_col):
        pl.semaphore_signal(
            barrier,
            inc=1,
            device_id={"row": to_row, "col": to_col},
            device_id_type=pl.DeviceIdType.MESH,
        )

    for d in range(1, n_row):
        greet(lax.rem(row + d, n_row), col)
    pl.when(col > 0)(lambda: greet(row, col - 1))
    pl.when(has_right)(lambda: greet(row, col + 1))
    work[...] = jnp.zeros_like(work)
    gram[...] = jnp.zeros_like(gram)
    inner = (col > 0) & has_right
    pl.semaphore_wait(barrier, n_row + inner.astype(jnp.int32))

    @pl.when(col < 2)
    def _():
        load_own(0).wait()

    @pl.when(col == 0)
    def _():
        @pl.loop(0, count)
        def _(c):
            send(0, 0, c).start()

    @pl.when(col == 1)
    def _():
        @pl.loop(0, count)
        def _(c):
            pl.when(has_right)(send(0, 1, c).start)
            send(1, 1, c).start()

    for b in range(blocks):
        load(b).wait()

    @pl.when(col == 0)
    def _():
        @pl.loop(0, count)
        def _(c):
            mine = wide[0, span(c), :]
            gram[0, :, :LANES] += dot_exact(mine, mine, 0, 0)

        scatter_start(2)
        scatter_finish(2)
        gather_finish(2)
        first = lower_inverse(gram_total[0, :, :LANES])
        factors[0] = first
        send_factor(0).start()

        @pl.loop(0, count)
        def _(c):
            send(1, 1, c).wait_recv()
            other = wide[1, span(c), :]
            pair = jnp.concatenate([wide[0, span(c), :], other], axis=1)
            gram[1] += dot_exact(other, pair, 0, 0)

        def multiply(start, stop):
            @pl.loop(start, stop)
            def _(c):
                pair = jnp.concatenate([wide[0, span(c), :], wide[1, span(c), :]], axis=1)
                work[...] += dot_exact(pair, window(c), 0, 0)

        scatter_start(3)
        for half in range(2):
            store_panel(half).start()
        multiply(0, count // 2)
        scatter_finish(3)
        multiply(count // 2, count)
        gather_finish(3)
        scatter_start(1)
        scatter_start(0)
        coupling = dot_exact(first, gram_total[1, :, :LANES], 1, 1)
        schur = gram_total[1, :, LANES:] - dot_exact(coupling, coupling, 0, 0)
        carried = dot_exact(coupling, first, 0, 0)
        second = lower_inverse(schur)
        factors[1] = second
        send_factor(1).start()
        factors[2] = -dot_exact(second, carried, 1, 0)
        send_factor(2).start()
        for stage in (1, 0):
            scatter_finish(stage)
        for stage in (1, 0):
            gather_finish(stage)
        for half in range(2):
            store_panel(half).wait()
        for stage in range(4):
            settle(stage)

        @pl.loop(0, count)
        def _(c):
            send(0, 0, c).wait_send()

        for which in range(3):
            send_factor(which).wait_send()

    @pl.when(col >= 1)
    def _():
        for half in (1, 0):

            @pl.loop(0, count)
            def _(c):
                if half == 1:

                    @pl.when(col >= 2)
                    def _():
                        send(0, 1, c).wait_recv()
                        pl.when(has_right)(send(0, 1, c).start)

                else:
                    send(0, 0, c).wait_recv()
                    pl.when(has_right)(send(0, 0, c).start)
                    pl.when(c == count // 2)(lambda: scatter_finish(1))
                here = pl.ds(half * LANES, LANES)
                work[here, :] += dot_exact(wide[half, span(c), :], window(c), 0, 0)

            scatter_start(half)
            store_panel(half).start()

        scatter_finish(0)
        for which in range(3):
            send_factor(which).wait_recv()
            pl.when(has_right)(send_factor(which).start)
        gather_finish(1)
        gather_finish(0)
        for half in range(2):
            store_panel(half).wait()
        for stage in (1, 0):
            settle(stage)

        @pl.when(col == 1)
        def _():
            @pl.loop(0, count)
            def _(c):
                send(1, 1, c).wait_send()

        @pl.when(has_right)
        def _():
            @pl.loop(0, count)
            def _(c):
                for half in range(2):
                    send(0, half, c).wait_send()

            for which in range(3):
                send_factor(which).wait_send()

    summed[...] = total[...]
    inverse[:LANES, :LANES] = factors[0]
    inverse[:LANES, LANES:] = jnp.zeros((LANES, LANES), jnp.float32)
    inverse[LANES:, :LANES] = factors[2]
    inverse[LANES:, LANES:] = factors[1]


def stream(matrix):
    rows, blocks, _, width = matrix.shape
    n_row = lax.axis_size("row")
    n_col = lax.axis_size("col")
    owners = min(n_row, 16)
    piece = LANES // owners
    chunk = 256
    count = rows // chunk
    columns = blocks * width
    sem = pltpu.SemaphoreType.DMA
    vmem = pl.BlockSpec(memory_space=pltpu.VMEM)
    hbm = pl.BlockSpec(memory_space=pl.ANY)

    def floats(*shape):
        return pltpu.VMEM(shape, jnp.float32)

    return pl.pallas_call(
        functools.partial(stream_kernel, n_row, n_col, owners, chunk),
        out_shape=(
            floats(blocks, rows, width),
            floats(2, rows, width),
            jax.ShapeDtypeStruct((2 * width, columns), jnp.float32),
            jax.ShapeDtypeStruct((2 * width, 2 * width), jnp.float32),
        ),
        in_specs=[hbm],
        out_specs=(vmem, vmem, vmem, vmem),
        scratch_shapes=[
            floats(2, rows, width),
            floats(2 * width, columns),
            floats(2 * width, columns),
            floats(2, width, 2 * width),
            floats(2, width, 2 * width),
            floats(2, n_row, piece, columns),
            floats(2, n_row, piece, 2 * width),
            floats(3, width, width),
            sem((blocks,)),
            sem,
            sem((2,)),
            sem((2, count)),
            sem((2, 2, count)),
            sem((3,)),
            sem((3,)),
            sem((4, n_row)),
            sem((4, n_row)),
            sem((4, n_row)),
            sem((4, n_row)),
        ],
        compiler_params=pltpu.CompilerParams(
            collective_id=0, has_side_effects=True, vmem_limit_bytes=STREAM_VMEM_LIMIT
        ),
        name="stream",
    )(matrix)


def per_device(matrix):
    local, panel, summed, inverse = stream(matrix)
    total_rows = matrix.shape[0] * lax.axis_size("row")
    return update(local, panel, summed, inverse, total_rows)


def solution(mesh):
    return jax.shard_map(
        per_device,
        mesh=mesh,
        in_specs=(P("row", None, "col", None),),
        out_specs=(P(None, None, "col", None), P("row", None, "col", None)),
        check_vma=False,
    )
```
